512 devices in a mesh: ctx: 32 (over y, x), head: 16 (over z, core).
Axes of the slice: x: 4, y: 8, z: 8, core: 2. Of those that a mesh axis runs over, the one named last changes fastest.
Arguments:
- tokens_x: bfloat16 [16384, 8192], P('ctx', 'head'), may hold values from -121 to 121
- raw_dt: float32 [128, 16384], P('head', 'ctx'), may hold values from -4 to 4
- in_b: bfloat16 [16384, 128], P('ctx'), may hold values from -0.5 to 0.5
- in_c: bfloat16 [16384, 128], P('ctx'), may hold values from -0.5 to 0.5
- decay_rate: float32 [128], P('head'), may hold values from 1.2207031e-06 to 2
- skip_gain: float32 [128], P('head'), may hold values from 0.5 to 1.5
- step_bias: float32 [128], P('head'), may hold values from -5 to -3
- grad_y: bfloat16 [16384, 8192], P('ctx', 'head'), may hold values from -121 to 121
Outputs:
- grad_x: bfloat16 [16384, 8192], P('ctx', 'head')
- grad_raw_dt: float32 [128, 16384], P('head', 'ctx')
- grad_b: float32 [16384, 128], P('ctx')
- grad_c: float32 [16384, 128], P('ctx')
- grad_rate: float32 [128], P('head')
- grad_skip: float32 [128], P('head')
- grad_bias: float32 [128], P('head')
The draws below stay inside these ranges and needn't reach their ends.
All inputs are finite; a program needn't handle non-finite values.
Results may differ from the reference program's by a relative error of at most 0.001.
Values sent between devices are 32-bit elements; how exact they have to be, the bound alone decides.
No kernel may reach another device: no remote copies, remote signals or barrier semaphores. Data moves between devices by JAX's collectives and lax.ppermute only.
A program may use at most 64 MiB of HBM per device.

```python
import math
import jax
import jax.numpy as jnp
from jax import lax

HEADS = 128
HEAD_DIM = 64
STATE = 128
BLOCK = 256
TOK_DEV = 512
TOKENS = 16384


rise_level = 3.0


def head_kinds(key):
    kind_pick = jax.random.randint(jax.random.fold_in(key, 101), (HEADS,), 0, 8)
    balanced = kind_pick < 2
    quiet_heads = (kind_pick >= 2) & (kind_pick < 5)
    return (balanced, quiet_heads)


def bias_values(key):
    return jax.random.uniform(jax.random.fold_in(key, 102), (HEADS,), jnp.float32, -5.0, -3.0)


def column_spread(key, direction):
    balanced, quiet_heads = head_kinds(key)
    position = jnp.arange(TOKENS, dtype=jnp.float32) / max(TOKENS - 1, 1)
    level_curve = jnp.exp(direction * rise_level * (1.0 - 2.0 * position))
    column_scale = jnp.where(balanced[None, :], level_curve[:, None], 1.0)
    return jnp.repeat(column_scale, HEAD_DIM, axis=1)


def noise_field(noise_key):
    array_shape = (TOKENS, HEADS * HEAD_DIM)
    noise_values = jnp.clip(jax.random.normal(noise_key, array_shape, jnp.float32), -6.0, 6.0)
    return noise_values


def draw_tokens_x(key, part):
    return (noise_field(jax.random.fold_in(key, 105)) * column_spread(key, 1.0)).astype(jnp.bfloat16)


def draw_grad_y(key, part):
    return (noise_field(jax.random.fold_in(key, 106)) * column_spread(key, -1.0)).astype(jnp.bfloat16)


def draw_step_bias(key, part):
    return bias_values(key)


def draw_decay_rate(key, part):
    balanced, quiet_heads = head_kinds(key)
    head_bias = bias_values(key)
    pieces = TOKENS // TOK_DEV
    mean_step = TOK_DEV * jnp.exp(head_bias + 0.5)
    draw_keys = jax.random.split(jax.random.fold_in(key, 103), 3)
    drawn_rate = jnp.exp(jax.random.uniform(draw_keys[0], (HEADS,), jnp.float32, math.log(1.0 / (50 * TOKENS)), math.log(1.5)))
    growth = 2.0 * rise_level / max(pieces - 1, 1)
    balanced_rate = jax.random.uniform(draw_keys[1], (HEADS,), jnp.float32, 1.3, 1.7) * growth / mean_step
    quiet_rate = jnp.exp(jax.random.uniform(draw_keys[2], (HEADS,), jnp.float32, math.log(0.7), math.log(2.5))) / mean_step
    return jnp.where(balanced, balanced_rate, jnp.where(quiet_heads, quiet_rate, drawn_rate))


def draw_raw_dt(key, part):
    balanced, quiet_heads = head_kinds(key)
    draw_keys = jax.random.split(jax.random.fold_in(key, 104), 4)
    outside = jnp.clip(jax.random.normal(draw_keys[0], (HEADS, TOKENS), jnp.float32), -4.0, 4.0)
    inside = jax.random.uniform(draw_keys[1], (HEADS, TOKENS), jnp.float32, -4.0, -2.5)
    gap_start = jax.random.uniform(draw_keys[2], (HEADS, 1), jnp.float32, 0.1, 0.3) * TOKENS
    gap_end = jax.random.uniform(draw_keys[3], (HEADS, 1), jnp.float32, 0.7, 0.9) * TOKENS
    position = jnp.arange(TOKENS, dtype=jnp.float32)[None, :]
    in_gap = quiet_heads[:, None] & (position >= gap_start) & (position < gap_end)
    return jnp.where(in_gap, inside, outside)


def shard_levels(own_key, dims, cuts, least, high):
    level = 1.0
    for dim, parts in cuts:
        heights = jax.random.uniform(jax.random.fold_in(jax.random.fold_in(own_key, 6), dim), (parts,), jnp.float32, least / len(cuts), high / len(cuts))
        level = level * jnp.repeat(jnp.exp(heights), dims[dim] // parts).reshape((-1,) + (1,) * (len(dims) - 1 - dim))
    return level


def centred(key, shape, deviation, reach, shards=(), kind=jnp.bfloat16):
    entries = deviation * jax.random.normal(key, shape, jnp.float32)
    if shards:
        entries = entries * shard_levels(key, shape, shards, -0.22, 0.18)
    return jnp.clip(entries, -reach, reach).astype(kind)


def setup_inputs(seed: int = 0) -> dict:
    seeds = jax.random.split(jax.random.key(seed), 9)
    tokens_x = draw_tokens_x(jax.random.fold_in(seeds[8], 71), 0)
    raw_dt = draw_raw_dt(jax.random.fold_in(seeds[8], 71), 0)
    in_b = centred(seeds[2], (TOKENS, STATE), STATE ** -0.5, 0.5, ((0, 32),))
    in_c = centred(seeds[3], (TOKENS, STATE), STATE ** -0.5, 0.5, ((0, 32),))
    decay_rate = draw_decay_rate(jax.random.fold_in(seeds[8], 71), 0)
    skip_gain = jnp.clip(0.5 + 1.0 * jax.random.uniform(seeds[5], (HEADS,), jnp.float32) ** shard_levels(seeds[5], (HEADS,), ((0, 16),), -0.2, 0.2), 0.5, 1.5)
    step_bias = draw_step_bias(jax.random.fold_in(seeds[8], 71), 0)
    grad_y = draw_grad_y(jax.random.fold_in(seeds[8], 71), 0)
    return dict(tokens_x=tokens_x, raw_dt=raw_dt, in_b=in_b, in_c=in_c, decay_rate=decay_rate, skip_gain=skip_gain, step_bias=step_bias, grad_y=grad_y)


def layer_forward(values, raw_dt, in_b, in_c, decay_rate, skip_gain, step_bias, start_state):
    token_count, head_count, head_size = values.shape
    state_size = in_b.shape[1]
    block_count = token_count // BLOCK
    step_sizes = jax.nn.softplus(raw_dt + step_bias[:, None])
    log_decay = -decay_rate[:, None] * step_sizes
    x_blocks = values.reshape(block_count, BLOCK, head_count, head_size)
    step_blocks = step_sizes.reshape(head_count, block_count, BLOCK).transpose(1, 0, 2)
    decay_blocks = log_decay.reshape(head_count, block_count, BLOCK).transpose(1, 0, 2)
    b_blocks = in_b.reshape(block_count, BLOCK, state_size)
    c_blocks = in_c.reshape(block_count, BLOCK, state_size)
    positions = jnp.arange(BLOCK)
    causal = positions[:, None] >= positions[None, :]

    def one_block(carry_state, pieces):
        x_block, step_block, decay_block, b_block, c_block = pieces
        cum_decay = jnp.cumsum(decay_block, axis=1)
        scores = jnp.dot(c_block, b_block.T, precision=lax.Precision.HIGHEST)
        log_gap = cum_decay[:, :, None] - cum_decay[:, None, :]
        mixing = jnp.where(causal[None], jnp.exp(jnp.where(causal[None], log_gap, 0.0)), 0.0)
        mixing = mixing * scores[None] * step_block[:, None, :]
        within = jnp.einsum('hts,shp->thp', mixing, x_block, precision=lax.Precision.HIGHEST)
        carried = jnp.einsum('hpn,tn->thp', carry_state, c_block, precision=lax.Precision.HIGHEST)
        carried = carried * jnp.exp(cum_decay).T[:, :, None]
        block_out = within + carried + skip_gain[None, :, None] * x_block
        end_decay = cum_decay[:, -1]
        state_weight = jnp.exp(end_decay[:, None] - cum_decay) * step_block
        weighted = x_block * state_weight.T[:, :, None]
        next_state = jnp.exp(end_decay)[:, None, None] * carry_state
        next_state = next_state + jnp.einsum('shp,sn->hpn', weighted, b_block, precision=lax.Precision.HIGHEST)
        return (next_state, block_out)
    final_state, block_outs = lax.scan(jax.checkpoint(one_block), start_state, (x_blocks, step_blocks, decay_blocks, b_blocks, c_blocks))
    return (block_outs.reshape(token_count, head_count, head_size), final_state)

def reference(tokens_x, raw_dt, in_b, in_c, decay_rate, skip_gain, step_bias, grad_y):
    values = tokens_x.astype(jnp.float32).reshape(TOKENS, HEADS, HEAD_DIM)
    b_full = in_b.astype(jnp.float32)
    c_full = in_c.astype(jnp.float32)
    cotangent = grad_y.astype(jnp.float32).reshape(TOKENS, HEADS, HEAD_DIM)
    start_state = jnp.zeros((HEADS, HEAD_DIM, STATE), jnp.float32)

    def forward(values, raw_dt, b_full, c_full, decay_rate, skip_gain, step_bias):
        outputs, final_state = layer_forward(values, raw_dt, b_full, c_full, decay_rate, skip_gain, step_bias, start_state)
        return outputs
    outputs, pullback = jax.vjp(forward, values, raw_dt, b_full, c_full, decay_rate, skip_gain, step_bias)
    grad_v, grad_raw, grad_b, grad_c, grad_rate, grad_skip, grad_bias = pullback(cotangent)
    grad_x = grad_v.reshape(TOKENS, HEADS * HEAD_DIM).astype(jnp.bfloat16)
    return (grad_x, grad_raw, grad_b, grad_c, grad_rate, grad_skip, grad_bias)
```

```python
import functools

import jax
import jax.numpy as jnp
from jax import lax
from jax.experimental import pallas as pl
from jax.experimental.pallas import tpu as pltpu
from jax.sharding import Mesh
from jax.sharding import PartitionSpec as P

F32, BF16 = jnp.float32, jnp.bfloat16
TOK, HEADS, DIM, STATE = 512, 8, 64, 128
COLS = HEADS * DIM
TB = 128
NB = TOK // TB
LOG2E = 1.4426950408889634
NT = (((1,), (1,)), ((), ()))
TN = (((0,), (0,)), ((), ()))
NN = (((1,), (0,)), ((), ()))


def mm(a, b, dims=NN):
    return lax.dot_general(a, b, dims, preferred_element_type=F32)


def split2(a):
    hi = a.astype(BF16)
    return hi, (a - hi.astype(F32)).astype(BF16)


def to_column(row):
    eye = lax.broadcasted_iota(jnp.int32, (HEADS, HEADS), 0) == lax.broadcasted_iota(
        jnp.int32, (HEADS, HEADS), 1
    )
    return jnp.sum(jnp.where(eye, row, 0.0), axis=1, keepdims=True)


def to_row(column):
    lane = lax.broadcasted_iota(jnp.int32, (HEADS, 128), 1)
    sub = lax.broadcasted_iota(jnp.int32, (HEADS, 128), 0)
    return jnp.sum(jnp.where(lane == sub, column, 0.0), axis=0, keepdims=True)


def member():
    lane = lax.broadcasted_iota(jnp.int32, (HEADS, COLS), 1)
    sub = lax.broadcasted_iota(jnp.int32, (HEADS, COLS), 0)
    return lane // DIM == sub


def over_channels(column):
    return jnp.sum(jnp.where(member(), column, 0.0), axis=0, keepdims=True)


def sum_channels(a):
    group = jnp.where(member(), 1.0, 0.0).astype(BF16)
    hi, lo = split2(a)
    return mm(group, hi, NT) + mm(group, lo, NT)


def expand(rows):
    hi = rows.astype(BF16).astype(F32)
    rest = rows - hi
    mid = rest.astype(BF16).astype(F32)
    parts = jnp.concatenate([hi, mid, rest - mid], axis=0).T.astype(BF16)
    lane = lax.broadcasted_iota(jnp.int32, (3 * HEADS, COLS), 1)
    sub = lax.broadcasted_iota(jnp.int32, (3 * HEADS, COLS), 0)
    spread = jnp.where(lane // DIM == lax.rem(sub, HEADS), 1.0, 0.0).astype(BF16)
    return mm(parts, spread)


def softplus(v):
    z = jnp.exp(-jnp.abs(v))
    u = 1.0 + z
    small = jnp.where(u == 1.0, z, jnp.log(u) * (z / jnp.where(u == 1.0, 1.0, u - 1.0)))
    return jnp.maximum(v, 0.0) + small


def decays(raw_ref, rate_ref, bias_ref):
    raw = raw_ref[...] + to_column(bias_ref[...])
    dt = softplus(raw)
    a = -(to_column(rate_ref[...]) * LOG2E) * dt
    stacked = jnp.concatenate([a[:, b * TB : (b + 1) * TB] for b in range(NB)], axis=0)
    s = lax.broadcasted_iota(jnp.int32, (TB, TB), 0)
    t = lax.broadcasted_iota(jnp.int32, (TB, TB), 1)
    upto = jnp.where(s <= t, 1.0, 0.0)
    cum = lax.dot_general(
        stacked, upto, NN, precision=lax.Precision.HIGHEST, preferred_element_type=F32
    )
    cum = [cum[b * HEADS : (b + 1) * HEADS] for b in range(NB)]
    total = [c[:, TB - 1 : TB] for c in cum]
    return raw, dt, cum, total


def head_weights(dt, cum, total):
    v, w = [], []
    for b in range(NB):
        v.append(jnp.exp2(cum[b] + sum(total[:b], jnp.zeros_like(total[0]))))
        rest = total[b] - cum[b] + sum(total[b + 1 :], jnp.zeros_like(total[0]))
        w.append(jnp.exp2(rest))
    return jnp.concatenate(v, axis=1), jnp.concatenate(w, axis=1) * dt


def k_states(
    x_ref, g_ref, b_ref, c_ref, raw_ref, rate_ref, bias_ref, send_ref, state_ref, decay_ref
):
    _, dt, cum, total = decays(raw_ref, rate_ref, bias_ref)
    v, w = head_weights(dt, cum, total)
    xw = split2(x_ref[...].astype(F32) * expand(w))
    gv = split2(g_ref[...].astype(F32) * expand(v))
    b, c = b_ref[...], c_ref[...]
    forward = mm(b, xw[0], TN) + mm(b, xw[1], TN)
    backward = mm(c, gv[0], TN) + mm(c, gv[1], TN)
    state_ref[...] = forward
    end = over_channels(jnp.exp2(sum(total)))
    decay_ref[...] = jnp.broadcast_to(end, (8, COLS))
    pieces = send_ref.shape[0]
    for j in range(pieces):
        source, k = (backward if j % 2 else forward), j // 2
        for q in range(4):
            send_ref[j, q * 8 : q * 8 + 8, :] = source[k * 8 : k * 8 + 8, q * 128 : q * 128 + 128]
            send_ref[j, 32 + q : 33 + q, :] = end[:, q * 128 : q * 128 + 128]
        send_ref[j, 36:40, :] = jnp.zeros((4, 128), F32)


def k_scan(odd_ref, got_ref, out_ref):
    pieces = got_ref.shape[0]
    odd = odd_ref[0]

    def step(i, acc):
        at = jnp.where(odd == 1, pieces - 1 - i, i)
        new = []
        for q in range(4):
            out_ref[at, q * 8 : q * 8 + 8, :] = acc[q]
            new.append(
                acc[q] * got_ref[at, 32 + q : 33 + q, :] + got_ref[at, q * 8 : q * 8 + 8, :]
            )
        return tuple(new)

    lax.fori_loop(0, pieces, step, tuple(jnp.zeros((8, 128), F32) for _ in range(4)))


def k_inner(
    x_ref, g_ref, b_ref, c_ref, raw_ref, rate_ref, bias_ref, skip_ref,
    dx_ref, rs_ref, cs_ref, db_ref, dc_ref, xh_ref, xl_ref, gh_ref, gl_ref, sk_ref,
    score_ref, ds_ref,
):
    _, dt, cum, total = decays(raw_ref, rate_ref, bias_ref)
    v, w = head_weights(dt, cum, total)
    x32, g32 = x_ref[...].astype(F32), g_ref[...].astype(F32)
    xh_ref[...], xl_ref[...] = split2(x32 * expand(w))
    gh_ref[...], gl_ref[...] = split2(g32 * expand(v))
    sk_ref[...] = jnp.broadcast_to(jnp.sum(x32 * g32, axis=0, keepdims=True), (8, COLS))
    score_ref[...] = mm(b_ref[...], c_ref[...], NT)
    rs_ref[...] = jnp.zeros_like(rs_ref)
    log_dt = jnp.log(dt) * LOG2E
    column = (jnp.concatenate(cum, axis=1) - log_dt).T
    s = lax.broadcasted_iota(jnp.int32, (TB, TB), 0)
    t = lax.broadcasted_iota(jnp.int32, (TB, TB), 1)
    causal = s <= t
    row = []
    for sb in range(NB):
        row.append(
            jnp.concatenate(
                [
                    cum[tb] + sum(total[sb:tb], jnp.zeros_like(total[0]))
                    for tb in range(sb, NB)
                ],
                axis=1,
            )
        )
    low = lax.broadcasted_iota(jnp.int32, (1, 128), 1) < DIM
    for pair in range(HEADS // 2):
        lanes = slice(pair * 128, pair * 128 + 128)
        zero = jnp.zeros((), BF16)
        gp = g_ref[:, lanes]
        g_of = (jnp.where(low, gp, zero), jnp.where(low, zero, gp))
        for sb in range(NB):
            at = slice(sb * TB, sb * TB + TB)
            after = slice(sb * TB, TOK)
            xs = x_ref[at, lanes]
            both = jnp.concatenate([jnp.where(low, xs, zero), jnp.where(low, zero, xs)], axis=0)
            q2 = mm(both, gp[after], NT)
            score = score_ref[at, after]
            ds, u = None, None
            for e in range(2):
                h = pair * 2 + e
                q = q2[e * TB : (e + 1) * TB]
                decay = jnp.exp2(row[sb][h : h + 1] - column[at, h : h + 1])
                first = jnp.where(causal, decay[:, :TB], 0.0)
                decay = jnp.concatenate([first, decay[:, TB:]], axis=1) if sb < NB - 1 else first
                part = decay * q
                mix = decay * score
                ds = part if ds is None else ds + part
                rs_ref[h : h + 1, after] += jnp.sum(mix * q, axis=0, keepdims=True)
                u2 = mm(jnp.concatenate(split2(mix), axis=0), g_of[e][after])
                u2 = u2[:TB] + u2[TB:]
                u = u2 if u is None else u + u2
            dx_ref[at, lanes] = u
            if pair == 0:
                ds_ref[at, after] = ds
            else:
                ds_ref[at, after] += ds
    for sb in range(NB):
        at, after = slice(sb * TB, sb * TB + TB), slice(sb * TB, TOK)
        d2 = mm(jnp.concatenate(split2(ds_ref[at, after]), axis=0), c_ref[after, :])
        db_ref[at, :] = d2[:TB] + d2[TB:]
        upto = slice(0, sb * TB + TB)
        hi, lo = split2(ds_ref[upto, at])
        dc_ref[at, :] = mm(hi, b_ref[upto, :], TN) + mm(lo, b_ref[upto, :], TN)
    u = dx_ref[...]
    cs_ref[...] = sum_channels(x32 * u)
    dx_ref[...] = u + g32 * over_channels(to_column(skip_ref[...]))


def join(got_ref, odd):
    return jnp.concatenate(
        [
            jnp.concatenate(
                [got_ref[2 * k + odd, q * 8 : q * 8 + 8, :] for q in range(4)], axis=1
            )
            for k in range(got_ref.shape[0] // 2)
        ],
        axis=0,
    )


def k_proj(core_ref, got_ref, xh_ref, xl_ref, gh_ref, gl_ref, db_ref, dc_ref, keep_ref, send_ref):
    def carried(state, hi_ref, lo_ref):
        sh, sl = split2(state)
        two = mm(hi_ref[...], jnp.concatenate([sh, sl], axis=0), NT)
        return two[:, :STATE] + two[:, STATE:] + mm(lo_ref[...], sh, NT)

    dc = dc_ref[...] + carried(join(got_ref, 0), gh_ref, gl_ref)
    db = db_ref[...] + carried(join(got_ref, 1), xh_ref, xl_ref)
    first = core_ref[0] == 0

    @pl.when(first)
    def _():
        keep_ref[...] = db
        send_ref[...] = dc

    @pl.when(jnp.logical_not(first))
    def _():
        keep_ref[...] = dc
        send_ref[...] = db


def k_close(
    got_ref, x_ref, g_ref, b_ref, c_ref, raw_ref, rate_ref, bias_ref,
    part_ref, rs_ref, cs_ref, state_ref, end_ref, sk_ref,
    dx_ref, draw_ref, param_ref,
):
    raw, dt, cum, total = decays(raw_ref, rate_ref, bias_ref)
    v, w = head_weights(dt, cum, total)
    before, after = join(got_ref, 0), join(got_ref, 1)
    sh, sl = split2(before)
    rh, rl = split2(after)
    carried_y = mm(c_ref[...], sh) + mm(c_ref[...], sl)
    carried_u = mm(b_ref[...], rh) + mm(b_ref[...], rl)
    dx_ref[...] = (part_ref[...] + carried_u * expand(w)).astype(BF16)
    rs = rs_ref[...] + v * sum_channels(g_ref[...].astype(F32) * carried_y)
    cs = cs_ref[...] + w * sum_channels(x_ref[...].astype(F32) * carried_u)
    last = before * end_ref[0:1, :] + state_ref[...]
    tail = jnp.sum(after * last, axis=0, keepdims=True)

    def per_head(row):
        return jnp.sum(jnp.where(member(), row, 0.0), axis=1, keepdims=True)

    dcum = rs - cs
    stacked = jnp.concatenate([dcum[:, b * TB : (b + 1) * TB] for b in range(NB)], axis=0)
    s = lax.broadcasted_iota(jnp.int32, (TB, TB), 0)
    t = lax.broadcasted_iota(jnp.int32, (TB, TB), 1)
    down = lax.dot_general(
        stacked,
        jnp.where(s >= t, 1.0, 0.0),
        NN,
        precision=lax.Precision.HIGHEST,
        preferred_element_type=F32,
    )
    later = per_head(tail)
    da = [None] * NB
    for b in reversed(range(NB)):
        here = down[b * HEADS : (b + 1) * HEADS]
        da[b] = here + later
        later = later + here[:, 0:1]
    da = jnp.concatenate(da, axis=1)
    draw = (cs / dt - da * to_column(rate_ref[...])) * (1.0 / (1.0 + jnp.exp(-raw)))
    draw_ref[...] = draw
    rate = to_row(-jnp.sum(da * dt, axis=1, keepdims=True))
    bias = to_row(jnp.sum(draw, axis=1, keepdims=True))
    skip = to_row(per_head(sk_ref[0:1, :]))
    rows = jnp.concatenate([rate, bias, skip, jnp.zeros((5, 128), F32)], axis=0)
    for j in range(param_ref.shape[0]):
        param_ref[j] = rows


VMEM = pl.BlockSpec(memory_space=pltpu.VMEM)
SMEM = pl.BlockSpec(memory_space=pltpu.SMEM)


def shape(dims, dtype=F32):
    return jax.ShapeDtypeStruct(dims, dtype)


def call(body, name, specs, outs, flops, scratch=()):
    return pl.pallas_call(
        body,
        in_specs=specs,
        out_specs=[VMEM] * len(outs),
        out_shape=outs,
        scratch_shapes=list(scratch),
        compiler_params=pltpu.CompilerParams(vmem_limit_bytes=48 << 20),
        cost_estimate=pl.CostEstimate(flops=flops, bytes_accessed=4 << 20, transcendentals=0),
        name=name,
    )


def states(pieces, *args):
    outs = [shape((pieces, 40, 128)), shape((STATE, COLS)), shape((8, COLS))]
    return call(k_states, "states", [VMEM] * 7, outs, 1 << 31)(*args)


def scan(odd, got):
    out = [shape((got.shape[0], 32, 128))]
    return call(k_scan, "scan", [SMEM, VMEM], out, 1 << 28)(odd, got)[0]


def inner(*args):
    outs = [
        shape((TOK, COLS)), shape((HEADS, TOK)), shape((HEADS, TOK)),
        shape((TOK, STATE)), shape((TOK, STATE)),
        shape((TOK, COLS), BF16), shape((TOK, COLS), BF16),
        shape((TOK, COLS), BF16), shape((TOK, COLS), BF16), shape((8, COLS)),
    ]
    scratch = [pltpu.VMEM((TOK, TOK), F32), pltpu.VMEM((TOK, TOK), F32)]
    return call(k_inner, "inner", [VMEM] * 8, outs, 1 << 33, scratch)(*args)


def proj(*args):
    outs = [shape((TOK, STATE)), shape((TOK, STATE))]
    return call(k_proj, "proj", [SMEM] + [VMEM] * 7, outs, 1 << 30)(*args)


def close(pieces, *args):
    outs = [shape((TOK, COLS), BF16), shape((HEADS, TOK)), shape((pieces, 8, 128))]
    return call(k_close, "close", [VMEM] * 14, outs, 1 << 31)(*args)


def on_device(tokens_x, raw_dt, in_b, in_c, decay_rate, skip_gain, step_bias, grad_y):
    ctx = ("y", "x")
    pieces = lax.axis_size(ctx)
    odd = lax.rem(lax.axis_index(ctx), 2).astype(jnp.int32).reshape(1)
    core = lax.axis_index("c").astype(jnp.int32).reshape(1)
    rate, skip, bias = (a.reshape(1, HEADS) for a in (decay_rate, skip_gain, step_bias))
    data = (tokens_x, grad_y, in_b, in_c, raw_dt, rate, bias)

    send, state, end = states(pieces, *data)
    got = lax.all_to_all(send, ctx, 0, 0)
    part, rs, cs, db, dc, xh, xl, gh, gl, sk = inner(*data, skip)
    got = lax.all_to_all(scan(odd, got), ctx, 0, 0)
    keep, send = proj(core, got, xh, xl, gh, gl, db, dc)
    swap = [(0, 1), (1, 0)]
    mine = keep + lax.ppermute(send, "c", swap)
    grad_x, grad_raw, params = close(pieces, got, *data, part, rs, cs, state, end, sk)
    ranks = lax.axis_size("z")
    mine = lax.all_to_all(mine.reshape(ranks, TOK // ranks, STATE), "z", 0, 0)
    mine = jnp.broadcast_to(jnp.sum(mine, axis=0)[None], mine.shape)
    mine = lax.all_to_all(mine, "z", 0, 0).reshape(TOK, STATE)
    other = lax.ppermute(mine, "c", swap)
    first = core[0] == 0
    grad_b, grad_c = jnp.where(first, mine, other), jnp.where(first, other, mine)
    params = jnp.sum(lax.all_to_all(params, ctx, 0, 0), axis=0)
    return (
        grad_x, grad_raw, grad_b, grad_c,
        params[0, :HEADS], params[2, :HEADS], params[1, :HEADS],
    )


def solution(mesh):
    fine = Mesh(mesh.devices.reshape(8, 4, 8, 2), ("y", "x", "z", "c"))
    ctx, head = ("y", "x"), ("z", "c")
    return jax.shard_map(
        on_device,
        mesh=fine,
        in_specs=(
            P(ctx, head), P(head, ctx), P(ctx, None), P(ctx, None),
            P(head), P(head), P(head), P(ctx, head),
        ),
        out_specs=(
            P(ctx, head), P(head, ctx), P(ctx, None), P(ctx, None),
            P(head), P(head), P(head),
        ),
        check_vma=False,
    )
```

```python
import functools

import jax
import jax.numpy as jnp
from jax import lax
from jax.experimental import pallas as pl
from jax.experimental.pallas import tpu as pltpu
from jax.sharding import Mesh
from jax.sharding import PartitionSpec as P

F32, BF16 = jnp.float32, jnp.bfloat16
TOK, HEADS, DIM, STATE = 512, 8, 64, 128
COLS = HEADS * DIM
TB = 128
NB = TOK // TB
LOG2E = 1.4426950408889634
NT = (((1,), (1,)), ((), ()))
TN = (((0,), (0,)), ((), ()))
NN = (((1,), (0,)), ((), ()))


def mm(a, b, dims=NN):
    return lax.dot_general(a, b, dims, preferred_element_type=F32)


def split2(a):
    hi = a.astype(BF16)
    return hi, (a - hi.astype(F32)).astype(BF16)


def to_column(row):
    eye = lax.broadcasted_iota(jnp.int32, (HEADS, HEADS), 0) == lax.broadcasted_iota(
        jnp.int32, (HEADS, HEADS), 1
    )
    return jnp.sum(jnp.where(eye, row, 0.0), axis=1, keepdims=True)


def to_row(column):
    lane = lax.broadcasted_iota(jnp.int32, (HEADS, 128), 1)
    sub = lax.broadcasted_iota(jnp.int32, (HEADS, 128), 0)
    return jnp.sum(jnp.where(lane == sub, column, 0.0), axis=0, keepdims=True)


def member():
    lane = lax.broadcasted_iota(jnp.int32, (HEADS, COLS), 1)
    sub = lax.broadcasted_iota(jnp.int32, (HEADS, COLS), 0)
    return lane // DIM == sub


def over_channels(column):
    return jnp.sum(jnp.where(member(), column, 0.0), axis=0, keepdims=True)


def sum_channels(a):
    group = jnp.where(member(), 1.0, 0.0).astype(BF16)
    hi, lo = split2(a)
    return mm(group, hi, NT) + mm(group, lo, NT)


def expand(rows):
    hi = rows.astype(BF16).astype(F32)
    rest = rows - hi
    mid = rest.astype(BF16).astype(F32)
    parts = jnp.concatenate([hi, mid, rest - mid], axis=0).T.astype(BF16)
    lane = lax.broadcasted_iota(jnp.int32, (3 * HEADS, COLS), 1)
    sub = lax.broadcasted_iota(jnp.int32, (3 * HEADS, COLS), 0)
    spread = jnp.where(lane // DIM == lax.rem(sub, HEADS), 1.0, 0.0).astype(BF16)
    return mm(parts, spread)


def expand_lanes(rows):
    hi = rows.astype(BF16)
    rest = rows - hi.astype(F32)
    mid = rest.astype(BF16)
    lo = (rest - mid.astype(F32)).astype(BF16)
    lane = lax.broadcasted_iota(jnp.int32, (128, COLS), 1)
    sub = lax.broadcasted_iota(jnp.int32, (128, COLS), 0)
    spread = jnp.where(lane // DIM == sub, 1.0, 0.0).astype(BF16)
    return mm(hi, spread) + mm(mid, spread) + mm(lo, spread)


def softplus(v):
    z = jnp.exp(-jnp.abs(v))
    u = 1.0 + z
    small = jnp.where(u == 1.0, z, jnp.log(u) * (z / jnp.where(u == 1.0, 1.0, u - 1.0)))
    return jnp.maximum(v, 0.0) + small


def decays(raw_ref, rate_ref, bias_ref):
    raw = raw_ref[...] + to_column(bias_ref[...])
    dt = softplus(raw)
    a = -(to_column(rate_ref[...]) * LOG2E) * dt
    stacked = jnp.concatenate([a[:, b * TB : (b + 1) * TB] for b in range(NB)], axis=0)
    s = lax.broadcasted_iota(jnp.int32, (TB, TB), 0)
    t = lax.broadcasted_iota(jnp.int32, (TB, TB), 1)
    upto = jnp.where(s <= t, 1.0, 0.0)
    cum = lax.dot_general(
        stacked, upto, NN, precision=lax.Precision.HIGHEST, preferred_element_type=F32
    )
    cum = [cum[b * HEADS : (b + 1) * HEADS] for b in range(NB)]
    total = [c[:, TB - 1 : TB] for c in cum]
    return raw, dt, cum, total


def head_weights(dt, cum, total):
    v, w = [], []
    for b in range(NB):
        v.append(jnp.exp2(cum[b] + sum(total[:b], jnp.zeros_like(total[0]))))
        rest = total[b] - cum[b] + sum(total[b + 1 :], jnp.zeros_like(total[0]))
        w.append(jnp.exp2(rest))
    return jnp.concatenate(v, axis=1), jnp.concatenate(w, axis=1) * dt


def k_states(*refs):
    sources, send_ref, local, sems = refs[:7], refs[7], refs[8:15], refs[15]
    x_ref, g_ref, b_ref, c_ref, raw_ref, rate_ref, bias_ref = local
    copies = [
        pltpu.make_async_copy(source, target, sems.at[i])
        for i, (source, target) in enumerate(zip(sources, local, strict=True))
    ]
    for copy in (*copies[4:], *copies[:4]):
        copy.start()
    for copy in copies[4:]:
        copy.wait()
    _, dt, cum, total = decays(raw_ref, rate_ref, bias_ref)
    v, w = head_weights(dt, cum, total)
    v, w = expand(v), expand(w)
    copies[0].wait()
    xw = split2(x_ref[...].astype(F32) * w)
    copies[1].wait()
    gv = split2(g_ref[...].astype(F32) * v)
    copies[2].wait()
    copies[3].wait()
    b, c = b_ref[...], c_ref[...]
    forward = mm(b, xw[0], TN) + mm(b, xw[1], TN)
    backward = mm(c, gv[0], TN) + mm(c, gv[1], TN)
    end = to_row(jnp.exp2(sum(total)))
    for j in range(send_ref.shape[0]):
        source, k = (backward if j % 2 else forward), j // 2
        for q in range(4):
            tile = source[k * 8 : k * 8 + 8, q * 128 : q * 128 + 128]
            send_ref[j, 0:1, q * 1024 : q * 1024 + 1024] = tile.reshape(1, 1024)
        send_ref[j, 0:1, 4096:4224] = end


def k_scan(odd_ref, got_ref, out_ref, decay_ref):
    pieces = got_ref.shape[0]
    odd = odd_ref[0]
    ends = jnp.concatenate([got_ref[j, 0:1, 4096:4224] for j in range(pieces)], axis=0)
    ends = expand_lanes(ends)
    for j in range(pieces):
        decay_ref[j] = ends[j : j + 1]

    def step(i, acc):
        at = jnp.where(odd == 1, pieces - 1 - i, i)
        new = []
        for q in range(4):
            out_ref[at, q * 8 : q * 8 + 8, :] = acc[q]
            new.append(
                acc[q] * decay_ref[at, 0:1, q * 128 : q * 128 + 128]
                + got_ref[at, 0:1, q * 1024 : q * 1024 + 1024].reshape(8, 128)
            )
        return tuple(new)

    lax.fori_loop(0, pieces, step, tuple(jnp.zeros((8, 128), F32) for _ in range(4)))


def k_inner(
    _, x_ref, g_ref, b_ref, c_ref, raw_ref, rate_ref, bias_ref, skip_ref,
    dx_ref, rs_ref, cs_ref, db_ref, dc_ref, xh_ref, xl_ref, gh_ref, gl_ref, sk_ref,
    state_ref, score_ref, ds_ref,
):
    _, dt, cum, total = decays(raw_ref, rate_ref, bias_ref)
    v, w = head_weights(dt, cum, total)
    x32, g32 = x_ref[...].astype(F32), g_ref[...].astype(F32)
    xh_ref[...], xl_ref[...] = split2(x32 * expand(w))
    gh_ref[...], gl_ref[...] = split2(g32 * expand(v))
    state_ref[...] = mm(b_ref[...], xh_ref[...], TN) + mm(b_ref[...], xl_ref[...], TN)
    sk_ref[...] = jnp.broadcast_to(jnp.sum(x32 * g32, axis=0, keepdims=True), (8, COLS))
    score_ref[...] = mm(b_ref[...], c_ref[...], NT)
    rs_ref[...] = jnp.zeros_like(rs_ref)
    log_dt = jnp.log(dt) * LOG2E
    column = (jnp.concatenate(cum, axis=1) - log_dt).T
    s = lax.broadcasted_iota(jnp.int32, (TB, TB), 0)
    t = lax.broadcasted_iota(jnp.int32, (TB, TB), 1)
    causal = s <= t
    row = []
    for sb in range(NB):
        row.append(
            jnp.concatenate(
                [
                    cum[tb] + sum(total[sb:tb], jnp.zeros_like(total[0]))
                    for tb in range(sb, NB)
                ],
                axis=1,
            )
        )
    low = lax.broadcasted_iota(jnp.int32, (1, 128), 1) < DIM
    for pair in range(HEADS // 2):
        lanes = slice(pair * 128, pair * 128 + 128)
        zero = jnp.zeros((), BF16)
        gp = g_ref[:, lanes]
        g_of = (jnp.where(low, gp, zero), jnp.where(low, zero, gp))
        for sb in range(NB):
            at = slice(sb * TB, sb * TB + TB)
            after = slice(sb * TB, TOK)
            xs = x_ref[at, lanes]
            both = jnp.concatenate([jnp.where(low, xs, zero), jnp.where(low, zero, xs)], axis=0)
            q2 = mm(both, gp[after], NT)
            score = score_ref[at, after]
            ds, u = None, None
            for e in range(2):
                h = pair * 2 + e
                q = q2[e * TB : (e + 1) * TB]
                decay = jnp.exp2(row[sb][h : h + 1] - column[at, h : h + 1])
                first = jnp.where(causal, decay[:, :TB], 0.0)
                decay = jnp.concatenate([first, decay[:, TB:]], axis=1) if sb < NB - 1 else first
                part = decay * q
                mix = decay * score
                ds = part if ds is None else ds + part
                rs_ref[h : h + 1, after] += jnp.sum(mix * q, axis=0, keepdims=True)
                u2 = mm(jnp.concatenate(split2(mix), axis=0), g_of[e][after])
                u2 = u2[:TB] + u2[TB:]
                u = u2 if u is None else u + u2
            dx_ref[at, lanes] = u
            if pair == 0:
                ds_ref[at, after] = ds
            else:
                ds_ref[at, after] += ds
    for sb in range(NB):
        at, after = slice(sb * TB, sb * TB + TB), slice(sb * TB, TOK)
        d2 = mm(jnp.concatenate(split2(ds_ref[at, after]), axis=0), c_ref[after, :])
        db_ref[at, :] = d2[:TB] + d2[TB:]
        upto = slice(0, sb * TB + TB)
        hi, lo = split2(ds_ref[upto, at])
        dc_ref[at, :] = mm(hi, b_ref[upto, :], TN) + mm(lo, b_ref[upto, :], TN)
    u = dx_ref[...]
    cs_ref[...] = sum_channels(x32 * u)
    dx_ref[...] = u + g32 * over_channels(to_column(skip_ref[...]))


def join(got_ref, odd):
    return jnp.concatenate(
        [
            jnp.concatenate(
                [got_ref[2 * k + odd, q * 8 : q * 8 + 8, :] for q in range(4)], axis=1
            )
            for k in range(got_ref.shape[0] // 2)
        ],
        axis=0,
    )


def k_proj(core_ref, got_ref, xh_ref, xl_ref, gh_ref, gl_ref, db_ref, dc_ref, keep_ref, send_ref):
    def carried(state, hi_ref, lo_ref):
        sh, sl = split2(state)
        two = mm(hi_ref[...], jnp.concatenate([sh, sl], axis=0), NT)
        return two[:, :STATE] + two[:, STATE:] + mm(lo_ref[...], sh, NT)

    dc = dc_ref[...] + carried(join(got_ref, 0), gh_ref, gl_ref)
    db = db_ref[...] + carried(join(got_ref, 1), xh_ref, xl_ref)
    first = core_ref[0] == 0

    @pl.when(first)
    def _():
        keep_ref[...] = db
        send_ref[...] = dc

    @pl.when(jnp.logical_not(first))
    def _():
        keep_ref[...] = dc
        send_ref[...] = db


def k_fold(got_ref, out_ref):
    total = got_ref[0]
    for i in range(1, got_ref.shape[0]):
        total = total + got_ref[i]
    for i in range(out_ref.shape[0]):
        out_ref[i] = total


def k_dx(got_ref, part_ref, b_ref, raw_ref, rate_ref, bias_ref, dx_ref):
    _, dt, cum, total = decays(raw_ref, rate_ref, bias_ref)
    _, w = head_weights(dt, cum, total)
    rh, rl = split2(join(got_ref, 1))
    carried_u = mm(b_ref[...], rh) + mm(b_ref[...], rl)
    dx_ref[...] = (part_ref[...] + carried_u * expand(w)).astype(BF16)


def k_params(
    got_ref, x_ref, g_ref, b_ref, c_ref, raw_ref, rate_ref, bias_ref,
    rs_ref, cs_ref, sk_ref, state_ref, draw_ref, param_ref,
):
    raw, dt, cum, total = decays(raw_ref, rate_ref, bias_ref)
    v, w = head_weights(dt, cum, total)
    before, after = join(got_ref, 0), join(got_ref, 1)
    sh, sl = split2(before)
    rh, rl = split2(after)
    carried_y = mm(c_ref[...], sh) + mm(c_ref[...], sl)
    carried_u = mm(b_ref[...], rh) + mm(b_ref[...], rl)
    rs = rs_ref[...] + v * sum_channels(g_ref[...].astype(F32) * carried_y)
    cs = cs_ref[...] + w * sum_channels(x_ref[...].astype(F32) * carried_u)
    last = before * over_channels(jnp.exp2(sum(total))) + state_ref[...]
    tail = jnp.sum(after * last, axis=0, keepdims=True)

    def per_head(row):
        return jnp.sum(jnp.where(member(), row, 0.0), axis=1, keepdims=True)

    dcum = rs - cs
    stacked = jnp.concatenate([dcum[:, b * TB : (b + 1) * TB] for b in range(NB)], axis=0)
    s = lax.broadcasted_iota(jnp.int32, (TB, TB), 0)
    t = lax.broadcasted_iota(jnp.int32, (TB, TB), 1)
    down = lax.dot_general(
        stacked,
        jnp.where(s >= t, 1.0, 0.0),
        NN,
        precision=lax.Precision.HIGHEST,
        preferred_element_type=F32,
    )
    later = per_head(tail)
    da = [None] * NB
    for b in reversed(range(NB)):
        here = down[b * HEADS : (b + 1) * HEADS]
        da[b] = here + later
        later = later + here[:, 0:1]
    da = jnp.concatenate(da, axis=1)
    draw = (cs / dt - da * to_column(rate_ref[...])) * (1.0 / (1.0 + jnp.exp(-raw)))
    draw_ref[...] = draw
    rate = to_row(-jnp.sum(da * dt, axis=1, keepdims=True))
    bias = to_row(jnp.sum(draw, axis=1, keepdims=True))
    skip = to_row(per_head(sk_ref[0:1, :]))
    lane = lax.broadcasted_iota(jnp.int32, (1, 128), 1)
    row = jnp.where(lane < HEADS, rate, 0.0)
    row = jnp.where(lane // HEADS == 1, pltpu.roll(bias, HEADS, 1), row)
    row = jnp.where(lane // HEADS == 2, pltpu.roll(skip, 2 * HEADS, 1), row)
    for j in range(param_ref.shape[0]):
        param_ref[j] = row


VMEM = pl.BlockSpec(memory_space=pltpu.VMEM)
HBM = pl.BlockSpec(memory_space=pltpu.HBM)
SMEM = pl.BlockSpec(memory_space=pltpu.SMEM)


def shape(dims, dtype=F32):
    return jax.ShapeDtypeStruct(dims, dtype)


def fetched(body, count, first, *refs):
    local, sems = refs[-1 - (count - first) : -1], refs[-1]
    copies = [
        pltpu.make_async_copy(source, target, sems.at[i])
        for i, (source, target) in enumerate(zip(refs[first:count], local, strict=True))
    ]
    for copy in copies:
        copy.start()
    for copy in copies:
        copy.wait()
    body(*refs[:first], *local, *refs[count : -1 - (count - first)])


def call(body, name, args, outs, flops, first=None, scratch=(), specs=()):
    count, scratch = len(args), list(scratch)
    first = count if first is None else first
    if first < count:
        scratch += [pltpu.VMEM(a.shape, a.dtype) for a in args[first:]]
        scratch.append(pltpu.SemaphoreType.DMA((count - first,)))
        args = [
            *args[:first],
            *(pltpu.with_memory_space_constraint(a, pltpu.HBM) for a in args[first:]),
        ]
        if first:
            body = functools.partial(fetched, body, count, first)
    specs = list(specs) + [VMEM] * (first - len(specs)) + [HBM] * (count - first)
    return pl.pallas_call(
        body,
        in_specs=specs,
        out_specs=[VMEM] * len(outs),
        out_shape=outs,
        scratch_shapes=scratch,
        compiler_params=pltpu.CompilerParams(vmem_limit_bytes=24 << 20),
        cost_estimate=pl.CostEstimate(flops=flops, bytes_accessed=4 << 20, transcendentals=0),
        name=name,
    )(*args)


def states(pieces, *args):
    return call(k_states, "states", args, [shape((pieces, 1, 4224))], 1 << 31, 0)[0]


def scan(odd, got):
    out = [shape((got.shape[0], 32, 128))]
    scratch = [pltpu.VMEM((got.shape[0], 1, COLS), F32)]
    return call(k_scan, "scan", (odd, got), out, 1 << 28, scratch=scratch, specs=[SMEM])[0]


def inner(odd, *args):
    outs = [
        shape((TOK, COLS)), shape((HEADS, TOK)), shape((HEADS, TOK)),
        shape((TOK, STATE)), shape((TOK, STATE)),
        shape((TOK, COLS), BF16), shape((TOK, COLS), BF16),
        shape((TOK, COLS), BF16), shape((TOK, COLS), BF16),
        shape((8, COLS)), shape((STATE, COLS)),
    ]
    scratch = [pltpu.VMEM((TOK, TOK), F32), pltpu.VMEM((TOK, TOK), F32)]
    return call(k_inner, "inner", (odd, *args), outs, 1 << 33, 1, scratch, [SMEM])


def proj(*args):
    outs = [shape((TOK, STATE)), shape((TOK, STATE))]
    return call(k_proj, "proj", args, outs, 1 << 30, specs=[SMEM])


def params(pieces, *args):
    outs = [shape((HEADS, TOK)), shape((pieces, 1, 128))]
    return call(k_params, "params", args, outs, 1 << 30, 1)


def dx(*args):
    return call(k_dx, "dx", args, [shape((TOK, COLS), BF16)], 1 << 30, 1)[0]


def fold(got):
    return call(k_fold, "fold", (got,), [shape(got.shape)], 1 << 20)[0]


def on_device(tokens_x, raw_dt, in_b, in_c, decay_rate, skip_gain, step_bias, grad_y):
    ctx = ("y", "x")
    pieces = lax.axis_size(ctx)
    odd = lax.rem(lax.axis_index(ctx), 2).astype(jnp.int32).reshape(1)
    core = lax.axis_index("c").astype(jnp.int32).reshape(1)
    rate, skip, bias = (a.reshape(1, HEADS) for a in (decay_rate, skip_gain, step_bias))
    data = (tokens_x, grad_y, in_b, in_c, raw_dt, rate, bias)

    send = states(pieces, *data)
    got = lax.all_to_all(send, ctx, 0, 0)
    part, rs, cs, db, dc, xh, xl, gh, gl, sk, state = inner(odd, *data, skip)
    got = lax.all_to_all(scan(odd, got), ctx, 0, 0)
    keep, send = proj(core, got, xh, xl, gh, gl, db, dc)
    swap = [(0, 1), (1, 0)]
    mine = keep + lax.ppermute(send, "c", swap)
    grad_raw, partial = params(pieces, got, *data, rs, cs, sk, state)
    ranks = lax.axis_size("z")
    mine = lax.all_to_all(mine.reshape(ranks, TOK // ranks, STATE), "z", 0, 0)
    grad_x = dx(got, part, in_b, raw_dt, rate, bias)
    mine = lax.all_to_all(fold(mine), "z", 0, 0).reshape(TOK, STATE)
    other = lax.ppermute(mine, "c", swap)
    partial = jnp.sum(lax.all_to_all(partial, ctx, 0, 0), axis=(0, 1))
    first = core[0] == 0
    grad_b, grad_c = jnp.where(first, mine, other), jnp.where(first, other, mine)
    return (
        grad_x, grad_raw, grad_b, grad_c,
        partial[:HEADS], partial[2 * HEADS : 3 * HEADS], partial[HEADS : 2 * HEADS],
    )


def solution(mesh):
    fine = Mesh(mesh.devices.reshape(8, 4, 8, 2), ("y", "x", "z", "c"))
    ctx, head = ("y", "x"), ("z", "c")
    return jax.shard_map(
        on_device,
        mesh=fine,
        in_specs=(
            P(ctx, head), P(head, ctx), P(ctx, None), P(ctx, None),
            P(head), P(head), P(head), P(ctx, head),
        ),
        out_specs=(
            P(ctx, head), P(head, ctx), P(ctx, None), P(ctx, None),
            P(head), P(head), P(head),
        ),
        check_vma=False,
    )
```

```python
import functools

import jax
import jax.numpy as jnp
from jax import lax
from jax.experimental import pallas as pl
from jax.experimental.pallas import tpu as pltpu
from jax.sharding import Mesh
from jax.sharding import PartitionSpec as P

F32, BF16 = jnp.float32, jnp.bfloat16
TOK, HEADS, DIM, STATE = 512, 8, 64, 128
COLS = HEADS * DIM
TB = 128
NB = TOK // TB
LOG2E = 1.4426950408889634
NT = (((1,), (1,)), ((), ()))
TN = (((0,), (0,)), ((), ()))
NN = (((1,), (0,)), ((), ()))


def mm(a, b, dims=NN):
    return lax.dot_general(a, b, dims, preferred_element_type=F32)


def split2(a):
    hi = a.astype(BF16)
    return hi, (a - hi.astype(F32)).astype(BF16)


def to_column(row):
    eye = lax.broadcasted_iota(jnp.int32, (HEADS, HEADS), 0) == lax.broadcasted_iota(
        jnp.int32, (HEADS, HEADS), 1
    )
    return jnp.sum(jnp.where(eye, row, 0.0), axis=1, keepdims=True)


def to_row(column):
    lane = lax.broadcasted_iota(jnp.int32, (HEADS, 128), 1)
    sub = lax.broadcasted_iota(jnp.int32, (HEADS, 128), 0)
    return jnp.sum(jnp.where(lane == sub, column, 0.0), axis=0, keepdims=True)


def member():
    lane = lax.broadcasted_iota(jnp.int32, (HEADS, COLS), 1)
    sub = lax.broadcasted_iota(jnp.int32, (HEADS, COLS), 0)
    return lane // DIM == sub


def block_sums(rows, reverse):
    stacked = jnp.concatenate([rows[:, b * TB : (b + 1) * TB] for b in range(NB)], axis=0)
    hi = stacked.astype(BF16)
    rest = stacked - hi.astype(F32)
    mid = rest.astype(BF16)
    lo = (rest - mid.astype(F32)).astype(BF16)
    s = lax.broadcasted_iota(jnp.int32, (TB, TB), 0)
    t = lax.broadcasted_iota(jnp.int32, (TB, TB), 1)
    ones = jnp.where(s >= t if reverse else s <= t, 1.0, 0.0).astype(BF16)
    sums = mm(jnp.concatenate([hi, mid, lo], axis=0), ones)
    n = NB * HEADS
    sums = sums[:n] + (sums[n : 2 * n] + sums[2 * n :])
    return [sums[b * HEADS : (b + 1) * HEADS] for b in range(NB)]


def over_channels(column):
    return jnp.sum(jnp.where(member(), column, 0.0), axis=0, keepdims=True)


def sum_channels(a):
    group = jnp.where(member(), 1.0, 0.0).astype(BF16)
    hi, lo = split2(a)
    return mm(group, hi, NT) + mm(group, lo, NT)


def expand(rows):
    hi = rows.astype(BF16).astype(F32)
    rest = rows - hi
    mid = rest.astype(BF16).astype(F32)
    parts = jnp.concatenate([hi, mid, rest - mid], axis=0).T.astype(BF16)
    lane = lax.broadcasted_iota(jnp.int32, (3 * HEADS, COLS), 1)
    sub = lax.broadcasted_iota(jnp.int32, (3 * HEADS, COLS), 0)
    spread = jnp.where(lane // DIM == lax.rem(sub, HEADS), 1.0, 0.0).astype(BF16)
    return mm(parts, spread)


def expand_lanes(rows):
    hi = rows.astype(BF16)
    rest = rows - hi.astype(F32)
    mid = rest.astype(BF16)
    lo = (rest - mid.astype(F32)).astype(BF16)
    lane = lax.broadcasted_iota(jnp.int32, (128, COLS), 1)
    sub = lax.broadcasted_iota(jnp.int32, (128, COLS), 0)
    spread = jnp.where(lane // DIM == sub, 1.0, 0.0).astype(BF16)
    return mm(hi, spread) + mm(mid, spread) + mm(lo, spread)


def softplus(v):
    z = jnp.exp(-jnp.abs(v))
    u = 1.0 + z
    small = jnp.where(u == 1.0, z, jnp.log(u) * (z / jnp.where(u == 1.0, 1.0, u - 1.0)))
    return jnp.maximum(v, 0.0) + small


def decays(raw_ref, rate_ref, bias_ref):
    raw = raw_ref[...] + to_column(bias_ref[...])
    dt = softplus(raw)
    a = -(to_column(rate_ref[...]) * LOG2E) * dt
    cum = block_sums(a, False)
    total = [c[:, TB - 1 : TB] for c in cum]
    return raw, dt, cum, total


def head_weights(dt, cum, total):
    v, w = [], []
    for b in range(NB):
        v.append(jnp.exp2(cum[b] + sum(total[:b], jnp.zeros_like(total[0]))))
        rest = total[b] - cum[b] + sum(total[b + 1 :], jnp.zeros_like(total[0]))
        w.append(jnp.exp2(rest))
    return jnp.concatenate(v, axis=1), jnp.concatenate(w, axis=1) * dt


def k_states(*refs):
    sources, send_ref, local, sems = refs[:7], refs[7], refs[8:15], refs[15]
    x_ref, g_ref, b_ref, c_ref, raw_ref, rate_ref, bias_ref = local
    copies = [
        pltpu.make_async_copy(source, target, sems.at[i])
        for i, (source, target) in enumerate(zip(sources, local, strict=True))
    ]
    for copy in (*copies[4:], *copies[:4]):
        copy.start()
    for copy in copies[4:]:
        copy.wait()
    _, dt, cum, total = decays(raw_ref, rate_ref, bias_ref)
    v, w = head_weights(dt, cum, total)
    v, w = expand(v), expand(w)
    copies[0].wait()
    xw = split2(x_ref[...].astype(F32) * w)
    copies[1].wait()
    gv = split2(g_ref[...].astype(F32) * v)
    copies[2].wait()
    copies[3].wait()
    b, c = b_ref[...], c_ref[...]
    forward = mm(b, xw[0], TN) + mm(b, xw[1], TN)
    backward = mm(c, gv[0], TN) + mm(c, gv[1], TN)
    end = to_row(jnp.exp2(sum(total)))
    for j in range(send_ref.shape[0]):
        source, k = (backward if j % 2 else forward), j // 2
        for q in range(4):
            tile = source[k * 8 : k * 8 + 8, q * 128 : q * 128 + 128]
            send_ref[j, 0:1, q * 1024 : q * 1024 + 1024] = tile.reshape(1, 1024)
        send_ref[j, 0:1, 4096:4224] = end


def k_scan(odd_ref, got_ref, out_ref, decay_ref):
    pieces = got_ref.shape[0]
    odd = odd_ref[0]
    ends = jnp.concatenate([got_ref[j, 0:1, 4096:4224] for j in range(pieces)], axis=0)
    ends = expand_lanes(ends)
    for j in range(pieces):
        decay_ref[j] = ends[j : j + 1]

    def step(i, acc):
        at = jnp.where(odd == 1, pieces - 1 - i, i)
        new = []
        for q in range(4):
            out_ref[at, 0:1, q * 1024 : q * 1024 + 1024] = acc[q].reshape(1, 1024)
            new.append(
                acc[q] * decay_ref[at, 0:1, q * 128 : q * 128 + 128]
                + got_ref[at, 0:1, q * 1024 : q * 1024 + 1024].reshape(8, 128)
            )
        return tuple(new)

    zero = tuple(jnp.zeros((8, 128), F32) for _ in range(4))
    lax.fori_loop(0, pieces, step, zero, unroll=8)


def k_inner(
    _, x_ref, g_ref, b_ref, c_ref, raw_ref, rate_ref, bias_ref, skip_ref,
    dx_ref, rs_ref, cs_ref, db_ref, dc_ref, xh_ref, xl_ref, gh_ref, gl_ref, sk_ref,
    state_ref, score_ref, ds_ref,
):
    _, dt, cum, total = decays(raw_ref, rate_ref, bias_ref)
    v, w = head_weights(dt, cum, total)
    x32, g32 = x_ref[...].astype(F32), g_ref[...].astype(F32)
    xh_ref[...], xl_ref[...] = split2(x32 * expand(w))
    gh_ref[...], gl_ref[...] = split2(g32 * expand(v))
    state_ref[...] = mm(b_ref[...], xh_ref[...], TN) + mm(b_ref[...], xl_ref[...], TN)
    sk_ref[...] = jnp.broadcast_to(jnp.sum(x32 * g32, axis=0, keepdims=True), (8, COLS))
    score_ref[...] = mm(b_ref[...], c_ref[...], NT)
    rs_ref[...] = jnp.zeros_like(rs_ref)
    log_dt = jnp.log(dt) * LOG2E
    column = (jnp.concatenate(cum, axis=1) - log_dt).T
    s = lax.broadcasted_iota(jnp.int32, (TB, TB), 0)
    t = lax.broadcasted_iota(jnp.int32, (TB, TB), 1)
    causal = s <= t
    row = []
    for sb in range(NB):
        row.append(
            jnp.concatenate(
                [
                    cum[tb] + sum(total[sb:tb], jnp.zeros_like(total[0]))
                    for tb in range(sb, NB)
                ],
                axis=1,
            )
        )
    low = lax.broadcasted_iota(jnp.int32, (1, 128), 1) < DIM
    for pair in range(HEADS // 2):
        lanes = slice(pair * 128, pair * 128 + 128)
        zero = jnp.zeros((), BF16)
        gp = g_ref[:, lanes]
        g_of = (jnp.where(low, gp, zero), jnp.where(low, zero, gp))
        for sb in range(NB):
            at = slice(sb * TB, sb * TB + TB)
            after = slice(sb * TB, TOK)
            xs = x_ref[at, lanes]
            both = jnp.concatenate([jnp.where(low, xs, zero), jnp.where(low, zero, xs)], axis=0)
            q2 = mm(both, gp[after], NT)
            score = score_ref[at, after]
            ds, u = None, None
            for e in range(2):
                h = pair * 2 + e
                q = q2[e * TB : (e + 1) * TB]
                decay = jnp.exp2(row[sb][h : h + 1] - column[at, h : h + 1])
                first = jnp.where(causal, decay[:, :TB], 0.0)
                decay = jnp.concatenate([first, decay[:, TB:]], axis=1) if sb < NB - 1 else first
                part = decay * q
                mix = decay * score
                ds = part if ds is None else ds + part
                rs_ref[h : h + 1, after] += jnp.sum(mix * q, axis=0, keepdims=True)
                u2 = mm(jnp.concatenate(split2(mix), axis=0), g_of[e][after])
                u2 = u2[:TB] + u2[TB:]
                u = u2 if u is None else u + u2
            dx_ref[at, lanes] = u
            if pair == 0:
                ds_ref[at, after] = ds
            else:
                ds_ref[at, after] += ds
    for sb in range(NB):
        at, after = slice(sb * TB, sb * TB + TB), slice(sb * TB, TOK)
        d2 = mm(jnp.concatenate(split2(ds_ref[at, after]), axis=0), c_ref[after, :])
        db_ref[at, :] = d2[:TB] + d2[TB:]
        upto = slice(0, sb * TB + TB)
        hi, lo = split2(ds_ref[upto, at])
        dc_ref[at, :] = mm(hi, b_ref[upto, :], TN) + mm(lo, b_ref[upto, :], TN)
    u = dx_ref[...]
    cs_ref[...] = sum_channels(x32 * u)
    dx_ref[...] = u + g32 * over_channels(to_column(skip_ref[...]))


def join(got_ref, odd):
    return jnp.concatenate(
        [
            jnp.concatenate(
                [
                    got_ref[2 * k + odd, 0:1, q * 1024 : q * 1024 + 1024].reshape(8, 128)
                    for q in range(4)
                ],
                axis=1,
            )
            for k in range(got_ref.shape[0] // 2)
        ],
        axis=0,
    )


def k_proj(core_ref, got_ref, xh_ref, xl_ref, gh_ref, gl_ref, db_ref, dc_ref, keep_ref, send_ref):
    def carried(state, hi_ref, lo_ref):
        sh, sl = split2(state)
        two = mm(hi_ref[...], jnp.concatenate([sh, sl], axis=0), NT)
        return two[:, :STATE] + two[:, STATE:] + mm(lo_ref[...], sh, NT)

    dc = dc_ref[...] + carried(join(got_ref, 0), gh_ref, gl_ref)
    db = db_ref[...] + carried(join(got_ref, 1), xh_ref, xl_ref)
    first = core_ref[0] == 0

    @pl.when(first)
    def _():
        keep_ref[...] = db
        send_ref[...] = dc

    @pl.when(jnp.logical_not(first))
    def _():
        keep_ref[...] = dc
        send_ref[...] = db


def k_fold(got_ref, out_ref):
    total = got_ref[0]
    for i in range(1, got_ref.shape[0]):
        total = total + got_ref[i]
    for i in range(out_ref.shape[0]):
        out_ref[i] = total


def k_dx(got_ref, part_ref, b_ref, raw_ref, rate_ref, bias_ref, dx_ref):
    _, dt, cum, total = decays(raw_ref, rate_ref, bias_ref)
    _, w = head_weights(dt, cum, total)
    rh, rl = split2(join(got_ref, 1))
    carried_u = mm(b_ref[...], rh) + mm(b_ref[...], rl)
    dx_ref[...] = (part_ref[...] + carried_u * expand(w)).astype(BF16)


def k_params(
    got_ref, x_ref, g_ref, b_ref, c_ref, raw_ref, rate_ref, bias_ref,
    rs_ref, cs_ref, sk_ref, state_ref, draw_ref, param_ref,
):
    raw, dt, cum, total = decays(raw_ref, rate_ref, bias_ref)
    v, w = head_weights(dt, cum, total)
    before, after = join(got_ref, 0), join(got_ref, 1)
    sh, sl = split2(before)
    rh, rl = split2(after)
    carried_y = mm(c_ref[...], sh) + mm(c_ref[...], sl)
    carried_u = mm(b_ref[...], rh) + mm(b_ref[...], rl)
    rs = rs_ref[...] + v * sum_channels(g_ref[...].astype(F32) * carried_y)
    cs = cs_ref[...] + w * sum_channels(x_ref[...].astype(F32) * carried_u)
    last = before * over_channels(jnp.exp2(sum(total))) + state_ref[...]
    tail = jnp.sum(after * last, axis=0, keepdims=True)

    def per_head(row):
        return jnp.sum(jnp.where(member(), row, 0.0), axis=1, keepdims=True)

    down = block_sums(rs - cs, True)
    later = per_head(tail)
    da = [None] * NB
    for b in reversed(range(NB)):
        here = down[b]
        da[b] = here + later
        later = later + here[:, 0:1]
    da = jnp.concatenate(da, axis=1)
    draw = (cs / dt - da * to_column(rate_ref[...])) * (1.0 / (1.0 + jnp.exp(-raw)))
    draw_ref[...] = draw
    rate = to_row(-jnp.sum(da * dt, axis=1, keepdims=True))
    bias = to_row(jnp.sum(draw, axis=1, keepdims=True))
    skip = to_row(per_head(sk_ref[0:1, :]))
    lane = lax.broadcasted_iota(jnp.int32, (1, 128), 1)
    row = jnp.where(lane < HEADS, rate, 0.0)
    row = jnp.where(lane // HEADS == 1, pltpu.roll(bias, HEADS, 1), row)
    row = jnp.where(lane // HEADS == 2, pltpu.roll(skip, 2 * HEADS, 1), row)
    for j in range(param_ref.shape[0]):
        param_ref[j] = row


VMEM = pl.BlockSpec(memory_space=pltpu.VMEM)
HBM = pl.BlockSpec(memory_space=pltpu.HBM)
SMEM = pl.BlockSpec(memory_space=pltpu.SMEM)


def shape(dims, dtype=F32):
    return jax.ShapeDtypeStruct(dims, dtype)


def fetched(body, count, first, *refs):
    local, sems = refs[-1 - (count - first) : -1], refs[-1]
    copies = [
        pltpu.make_async_copy(source, target, sems.at[i])
        for i, (source, target) in enumerate(zip(refs[first:count], local, strict=True))
    ]
    for copy in copies:
        copy.start()
    for copy in copies:
        copy.wait()
    body(*refs[:first], *local, *refs[count : -1 - (count - first)])


def call(body, name, args, outs, flops, first=None, scratch=(), specs=()):
    count, scratch = len(args), list(scratch)
    first = count if first is None else first
    if first < count:
        scratch += [pltpu.VMEM(a.shape, a.dtype) for a in args[first:]]
        scratch.append(pltpu.SemaphoreType.DMA((count - first,)))
        args = [
            *args[:first],
            *(pltpu.with_memory_space_constraint(a, pltpu.HBM) for a in args[first:]),
        ]
        if first:
            body = functools.partial(fetched, body, count, first)
    specs = list(specs) + [VMEM] * (first - len(specs)) + [HBM] * (count - first)
    return pl.pallas_call(
        body,
        in_specs=specs,
        out_specs=[VMEM] * len(outs),
        out_shape=outs,
        scratch_shapes=scratch,
        compiler_params=pltpu.CompilerParams(vmem_limit_bytes=24 << 20),
        cost_estimate=pl.CostEstimate(flops=flops, bytes_accessed=4 << 20, transcendentals=0),
        name=name,
    )(*args)


def states(pieces, *args):
    return call(k_states, "states", args, [shape((pieces, 1, 4224))], 1 << 31, 0)[0]


def scan(odd, got):
    out = [shape((got.shape[0], 1, 4096))]
    scratch = [pltpu.VMEM((got.shape[0], 1, COLS), F32)]
    return call(k_scan, "scan", (odd, got), out, 1 << 28, scratch=scratch, specs=[SMEM])[0]


def inner(odd, *args):
    outs = [
        shape((TOK, COLS)), shape((HEADS, TOK)), shape((HEADS, TOK)),
        shape((TOK, STATE)), shape((TOK, STATE)),
        shape((TOK, COLS), BF16), shape((TOK, COLS), BF16),
        shape((TOK, COLS), BF16), shape((TOK, COLS), BF16),
        shape((8, COLS)), shape((STATE, COLS)),
    ]
    scratch = [pltpu.VMEM((TOK, TOK), F32), pltpu.VMEM((TOK, TOK), F32)]
    return call(k_inner, "inner", (odd, *args), outs, 1 << 33, 1, scratch, [SMEM])


def proj(*args):
    outs = [shape((TOK, STATE)), shape((TOK, STATE))]
    return call(k_proj, "proj", args, outs, 1 << 30, specs=[SMEM])


def params(pieces, *args):
    outs = [shape((HEADS, TOK)), shape((pieces, 1, 128))]
    return call(k_params, "params", args, outs, 1 << 30, 1)


def dx(*args):
    return call(k_dx, "dx", args, [shape((TOK, COLS), BF16)], 1 << 30, 1)[0]


def fold(got):
    return call(k_fold, "fold", (got,), [shape(got.shape)], 1 << 20)[0]


def on_device(tokens_x, raw_dt, in_b, in_c, decay_rate, skip_gain, step_bias, grad_y):
    ctx = ("y", "x")
    pieces = lax.axis_size(ctx)
    odd = lax.rem(lax.axis_index(ctx), 2).astype(jnp.int32).reshape(1)
    core = lax.axis_index("c").astype(jnp.int32).reshape(1)
    rate, skip, bias = (a.reshape(1, HEADS) for a in (decay_rate, skip_gain, step_bias))
    data = (tokens_x, grad_y, in_b, in_c, raw_dt, rate, bias)

    send = states(pieces, *data)
    send, odd, core = lax.optimization_barrier((send, odd, core))
    got = lax.all_to_all(send, ctx, 0, 0)
    part, rs, cs, db, dc, xh, xl, gh, gl, sk, state = inner(odd, *data, skip)
    got = lax.all_to_all(scan(odd, got), ctx, 0, 0)
    keep, send = proj(core, got, xh, xl, gh, gl, db, dc)
    swap = [(0, 1), (1, 0)]
    mine = keep + lax.ppermute(send, "c", swap)
    grad_raw, partial = params(pieces, got, *data, rs, cs, sk, state)
    ranks = lax.axis_size("z")
    mine = lax.all_to_all(mine.reshape(ranks, TOK // ranks, STATE), "z", 0, 0)
    grad_x = dx(got, part, in_b, raw_dt, rate, bias)
    mine = lax.all_to_all(fold(mine), "z", 0, 0).reshape(TOK, STATE)
    other = lax.ppermute(mine, "c", swap)
    partial = jnp.sum(lax.all_to_all(partial, ctx, 0, 0), axis=(0, 1))
    first = core[0] == 0
    grad_b, grad_c = jnp.where(first, mine, other), jnp.where(first, other, mine)
    return (
        grad_x, grad_raw, grad_b, grad_c,
        partial[:HEADS], partial[2 * HEADS : 3 * HEADS], partial[HEADS : 2 * HEADS],
    )


def solution(mesh):
    fine = Mesh(mesh.devices.reshape(8, 4, 8, 2), ("y", "x", "z", "c"))
    ctx, head = ("y", "x"), ("z", "c")
    return jax.shard_map(
        on_device,
        mesh=fine,
        in_specs=(
            P(ctx, head), P(head, ctx), P(ctx, None), P(ctx, None),
            P(head), P(head), P(head), P(ctx, head),
        ),
        out_specs=(
            P(ctx, head), P(head, ctx), P(ctx, None), P(ctx, None),
            P(head), P(head), P(head),
        ),
        check_vma=False,
    )
```

```python
import functools

import jax
import jax.numpy as jnp
from jax import lax
from jax.experimental import pallas as pl
from jax.experimental.pallas import tpu as pltpu
from jax.sharding import Mesh
from jax.sharding import PartitionSpec as P

F32, BF16 = jnp.float32, jnp.bfloat16
TOK, HEADS, DIM, STATE = 512, 8, 64, 128
COLS = HEADS * DIM
TB = 128
NB = TOK // TB
LOG2E = 1.4426950408889634
NT = (((1,), (1,)), ((), ()))
TN = (((0,), (0,)), ((), ()))
NN = (((1,), (0,)), ((), ()))


def mm(a, b, dims=NN):
    return lax.dot_general(a, b, dims, preferred_element_type=F32)


def split2(a):
    hi = a.astype(BF16)
    return hi, (a - hi.astype(F32)).astype(BF16)


def to_column(row):
    eye = lax.broadcasted_iota(jnp.int32, (HEADS, HEADS), 0) == lax.broadcasted_iota(
        jnp.int32, (HEADS, HEADS), 1
    )
    return jnp.sum(jnp.where(eye, row, 0.0), axis=1, keepdims=True)


def to_row(column):
    lane = lax.broadcasted_iota(jnp.int32, (HEADS, 128), 1)
    sub = lax.broadcasted_iota(jnp.int32, (HEADS, 128), 0)
    return jnp.sum(jnp.where(lane == sub, column, 0.0), axis=0, keepdims=True)


def member():
    lane = lax.broadcasted_iota(jnp.int32, (HEADS, COLS), 1)
    sub = lax.broadcasted_iota(jnp.int32, (HEADS, COLS), 0)
    return lane // DIM == sub


def block_sums(rows, reverse):
    stacked = jnp.concatenate([rows[:, b * TB : (b + 1) * TB] for b in range(NB)], axis=0)
    hi = stacked.astype(BF16)
    rest = stacked - hi.astype(F32)
    mid = rest.astype(BF16)
    lo = (rest - mid.astype(F32)).astype(BF16)
    s = lax.broadcasted_iota(jnp.int32, (TB, TB), 0)
    t = lax.broadcasted_iota(jnp.int32, (TB, TB), 1)
    ones = jnp.where(s >= t if reverse else s <= t, 1.0, 0.0).astype(BF16)
    sums = mm(jnp.concatenate([hi, mid, lo], axis=0), ones)
    n = NB * HEADS
    sums = sums[:n] + (sums[n : 2 * n] + sums[2 * n :])
    return [sums[b * HEADS : (b + 1) * HEADS] for b in range(NB)]


def over_channels(column):
    return jnp.sum(jnp.where(member(), column, 0.0), axis=0, keepdims=True)


def sum_channels(a):
    group = jnp.where(member(), 1.0, 0.0).astype(BF16)
    hi, lo = split2(a)
    return mm(group, hi, NT) + mm(group, lo, NT)


def expand(rows):
    hi = rows.astype(BF16).astype(F32)
    rest = rows - hi
    mid = rest.astype(BF16).astype(F32)
    parts = jnp.concatenate([hi, mid, rest - mid], axis=0).T.astype(BF16)
    lane = lax.broadcasted_iota(jnp.int32, (3 * HEADS, COLS), 1)
    sub = lax.broadcasted_iota(jnp.int32, (3 * HEADS, COLS), 0)
    spread = jnp.where(lane // DIM == lax.rem(sub, HEADS), 1.0, 0.0).astype(BF16)
    return mm(parts, spread)


def expand_lanes(rows):
    hi = rows.astype(BF16)
    rest = rows - hi.astype(F32)
    mid = rest.astype(BF16)
    lo = (rest - mid.astype(F32)).astype(BF16)
    lane = lax.broadcasted_iota(jnp.int32, (128, COLS), 1)
    sub = lax.broadcasted_iota(jnp.int32, (128, COLS), 0)
    spread = jnp.where(lane // DIM == sub, 1.0, 0.0).astype(BF16)
    return mm(hi, spread) + mm(mid, spread) + mm(lo, spread)


def softplus(v):
    z = jnp.exp(-jnp.abs(v))
    u = 1.0 + z
    small = jnp.where(u == 1.0, z, jnp.log(u) * (z / jnp.where(u == 1.0, 1.0, u - 1.0)))
    return jnp.maximum(v, 0.0) + small


def decays(raw_ref, rate_ref, bias_ref):
    raw = raw_ref[...] + to_column(bias_ref[...])
    dt = softplus(raw)
    a = -(to_column(rate_ref[...]) * LOG2E) * dt
    cum = block_sums(a, False)
    total = [c[:, TB - 1 : TB] for c in cum]
    return raw, dt, cum, total


def head_weights(dt, cum, total):
    v, w = [], []
    for b in range(NB):
        v.append(jnp.exp2(cum[b] + sum(total[:b], jnp.zeros_like(total[0]))))
        rest = total[b] - cum[b] + sum(total[b + 1 :], jnp.zeros_like(total[0]))
        w.append(jnp.exp2(rest))
    return jnp.concatenate(v, axis=1), jnp.concatenate(w, axis=1) * dt


def k_states(*refs):
    sources, send_ref, local, sems = refs[:7], refs[7], refs[8:15], refs[15]
    x_ref, g_ref, b_ref, c_ref, raw_ref, rate_ref, bias_ref = local
    copies = [
        pltpu.make_async_copy(source, target, sems.at[i])
        for i, (source, target) in enumerate(zip(sources, local, strict=True))
    ]
    for copy in (*copies[4:], *copies[:4]):
        copy.start()
    for copy in copies[4:]:
        copy.wait()
    _, dt, cum, total = decays(raw_ref, rate_ref, bias_ref)
    v, w = head_weights(dt, cum, total)
    v, w = expand(v), expand(w)
    copies[0].wait()
    xw = split2(x_ref[...].astype(F32) * w)
    copies[1].wait()
    gv = split2(g_ref[...].astype(F32) * v)
    copies[2].wait()
    copies[3].wait()
    b, c = b_ref[...], c_ref[...]
    forward = mm(b, xw[0], TN) + mm(b, xw[1], TN)
    backward = mm(c, gv[0], TN) + mm(c, gv[1], TN)
    end = to_row(jnp.exp2(sum(total)))
    for j in range(send_ref.shape[0]):
        source, k = (backward if j % 2 else forward), j // 2
        for q in range(4):
            tile = source[k * 8 : k * 8 + 8, q * 128 : q * 128 + 128]
            send_ref[j, 0:1, q * 1024 : q * 1024 + 1024] = tile.reshape(1, 1024)
        send_ref[j, 0:1, 4096:4224] = end


def k_scan(odd_ref, got_ref, out_ref, decay_ref):
    pieces = got_ref.shape[0]
    odd = odd_ref[0]
    ends = jnp.concatenate([got_ref[j, 0:1, 4096:4224] for j in range(pieces)], axis=0)
    ends = expand_lanes(ends)
    for j in range(pieces):
        decay_ref[j] = ends[j : j + 1]

    def step(i, acc):
        at = jnp.where(odd == 1, pieces - 1 - i, i)
        new = []
        for q in range(4):
            out_ref[at, 0:1, q * 1024 : q * 1024 + 1024] = acc[q].reshape(1, 1024)
            new.append(
                acc[q] * decay_ref[at, 0:1, q * 128 : q * 128 + 128]
                + got_ref[at, 0:1, q * 1024 : q * 1024 + 1024].reshape(8, 128)
            )
        return tuple(new)

    zero = tuple(jnp.zeros((8, 128), F32) for _ in range(4))
    lax.fori_loop(0, pieces, step, zero, unroll=8)


def k_inner(
    _, x_ref, g_ref, b_ref, c_ref, raw_ref, rate_ref, bias_ref, skip_ref,
    dx_ref, rs_ref, cs_ref, db_ref, dc_ref, xh_ref, xl_ref, gh_ref, gl_ref, sk_ref,
    state_ref, score_ref, ds_ref,
):
    _, dt, cum, total = decays(raw_ref, rate_ref, bias_ref)
    v, w = head_weights(dt, cum, total)
    x32, g32 = x_ref[...].astype(F32), g_ref[...].astype(F32)
    xh_ref[...], xl_ref[...] = split2(x32 * expand(w))
    gh_ref[...], gl_ref[...] = split2(g32 * expand(v))
    state_ref[...] = mm(b_ref[...], xh_ref[...], TN) + mm(b_ref[...], xl_ref[...], TN)
    sk_ref[...] = jnp.broadcast_to(jnp.sum(x32 * g32, axis=0, keepdims=True), (8, COLS))
    score_ref[...] = mm(b_ref[...], c_ref[...], NT)
    rs_ref[...] = jnp.zeros_like(rs_ref)
    log_dt = jnp.log(dt) * LOG2E
    column = (jnp.concatenate(cum, axis=1) - log_dt).T
    s = lax.broadcasted_iota(jnp.int32, (TB, TB), 0)
    t = lax.broadcasted_iota(jnp.int32, (TB, TB), 1)
    causal = s <= t
    row = []
    for sb in range(NB):
        row.append(
            jnp.concatenate(
                [
                    cum[tb] + sum(total[sb:tb], jnp.zeros_like(total[0]))
                    for tb in range(sb, NB)
                ],
                axis=1,
            )
        )
    low = lax.broadcasted_iota(jnp.int32, (1, 128), 1) < DIM
    for pair in range(HEADS // 2):
        lanes = slice(pair * 128, pair * 128 + 128)
        zero = jnp.zeros((), BF16)
        gp = g_ref[:, lanes]
        g_of = (jnp.where(low, gp, zero), jnp.where(low, zero, gp))
        for sb in range(NB):
            at = slice(sb * TB, sb * TB + TB)
            after = slice(sb * TB, TOK)
            xs = x_ref[at, lanes]
            both = jnp.concatenate([jnp.where(low, xs, zero), jnp.where(low, zero, xs)], axis=0)
            q2 = mm(both, gp[after], NT)
            score = score_ref[at, after]
            ds, u = None, None
            for e in range(2):
                h = pair * 2 + e
                q = q2[e * TB : (e + 1) * TB]
                decay = jnp.exp2(row[sb][h : h + 1] - column[at, h : h + 1])
                first = jnp.where(causal, decay[:, :TB], 0.0)
                decay = jnp.concatenate([first, decay[:, TB:]], axis=1) if sb < NB - 1 else first
                part = decay * q
                mix = decay * score
                ds = part if ds is None else ds + part
                rs_ref[h : h + 1, after] += jnp.sum(mix * q, axis=0, keepdims=True)
                u2 = mm(jnp.concatenate(split2(mix), axis=0), g_of[e][after])
                u2 = u2[:TB] + u2[TB:]
                u = u2 if u is None else u + u2
            dx_ref[at, lanes] = u
            if pair == 0:
                ds_ref[at, after] = ds
            else:
                ds_ref[at, after] += ds
    for sb in range(NB):
        at, after = slice(sb * TB, sb * TB + TB), slice(sb * TB, TOK)
        d2 = mm(jnp.concatenate(split2(ds_ref[at, after]), axis=0), c_ref[after, :])
        db_ref[at, :] = d2[:TB] + d2[TB:]
        upto = slice(0, sb * TB + TB)
        hi, lo = split2(ds_ref[upto, at])
        dc_ref[at, :] = mm(hi, b_ref[upto, :], TN) + mm(lo, b_ref[upto, :], TN)
    u = dx_ref[...]
    cs_ref[...] = sum_channels(x32 * u)
    dx_ref[...] = u + g32 * over_channels(to_column(skip_ref[...]))


def join(got_ref, odd):
    return jnp.concatenate(
        [
            jnp.concatenate(
                [
                    got_ref[2 * k + odd, 0:1, q * 1024 : q * 1024 + 1024].reshape(8, 128)
                    for q in range(4)
                ],
                axis=1,
            )
            for k in range(got_ref.shape[0] // 2)
        ],
        axis=0,
    )


def k_proj(mine, core_ref, got_ref, xh_ref, xl_ref, gh_ref, gl_ref, db_ref, dc_ref, out_ref):
    def carried(state, hi_ref, lo_ref):
        sh, sl = split2(state)
        two = mm(hi_ref[...], jnp.concatenate([sh, sl], axis=0), NT)
        return two[:, :STATE] + two[:, STATE:] + mm(lo_ref[...], sh, NT)

    for_b = (core_ref[0] == 0) if mine else (core_ref[0] != 0)

    @pl.when(for_b)
    def _():
        out_ref[...] = db_ref[...] + carried(join(got_ref, 1), xh_ref, xl_ref)

    @pl.when(jnp.logical_not(for_b))
    def _():
        out_ref[...] = dc_ref[...] + carried(join(got_ref, 0), gh_ref, gl_ref)


def k_fold(got_ref, out_ref):
    total = got_ref[0]
    for i in range(1, got_ref.shape[0]):
        total = total + got_ref[i]
    for i in range(out_ref.shape[0]):
        out_ref[i] = total


def k_dx(got_ref, part_ref, b_ref, raw_ref, rate_ref, bias_ref, dx_ref):
    _, dt, cum, total = decays(raw_ref, rate_ref, bias_ref)
    _, w = head_weights(dt, cum, total)
    rh, rl = split2(join(got_ref, 1))
    carried_u = mm(b_ref[...], rh) + mm(b_ref[...], rl)
    dx_ref[...] = (part_ref[...] + carried_u * expand(w)).astype(BF16)


def k_params(
    got_ref, x_ref, g_ref, b_ref, c_ref, raw_ref, rate_ref, bias_ref,
    rs_ref, cs_ref, sk_ref, state_ref, draw_ref, param_ref,
):
    raw, dt, cum, total = decays(raw_ref, rate_ref, bias_ref)
    v, w = head_weights(dt, cum, total)
    before, after = join(got_ref, 0), join(got_ref, 1)
    sh, sl = split2(before)
    rh, rl = split2(after)
    carried_y = mm(c_ref[...], sh) + mm(c_ref[...], sl)
    carried_u = mm(b_ref[...], rh) + mm(b_ref[...], rl)
    rs = rs_ref[...] + v * sum_channels(g_ref[...].astype(F32) * carried_y)
    cs = cs_ref[...] + w * sum_channels(x_ref[...].astype(F32) * carried_u)
    last = before * over_channels(jnp.exp2(sum(total))) + state_ref[...]
    tail = jnp.sum(after * last, axis=0, keepdims=True)

    def per_head(row):
        return jnp.sum(jnp.where(member(), row, 0.0), axis=1, keepdims=True)

    down = block_sums(rs - cs, True)
    later = per_head(tail)
    da = [None] * NB
    for b in reversed(range(NB)):
        here = down[b]
        da[b] = here + later
        later = later + here[:, 0:1]
    da = jnp.concatenate(da, axis=1)
    draw = (cs / dt - da * to_column(rate_ref[...])) * (1.0 / (1.0 + jnp.exp(-raw)))
    draw_ref[...] = draw
    rate = to_row(-jnp.sum(da * dt, axis=1, keepdims=True))
    bias = to_row(jnp.sum(draw, axis=1, keepdims=True))
    skip = to_row(per_head(sk_ref[0:1, :]))
    lane = lax.broadcasted_iota(jnp.int32, (1, 128), 1)
    row = jnp.where(lane < HEADS, rate, 0.0)
    row = jnp.where(lane // HEADS == 1, pltpu.roll(bias, HEADS, 1), row)
    row = jnp.where(lane // HEADS == 2, pltpu.roll(skip, 2 * HEADS, 1), row)
    for j in range(param_ref.shape[0]):
        param_ref[j] = row


VMEM = pl.BlockSpec(memory_space=pltpu.VMEM)
HBM = pl.BlockSpec(memory_space=pltpu.HBM)
SMEM = pl.BlockSpec(memory_space=pltpu.SMEM)


def shape(dims, dtype=F32):
    return jax.ShapeDtypeStruct(dims, dtype)


def fetched(body, count, first, *refs):
    local, sems = refs[-1 - (count - first) : -1], refs[-1]
    copies = [
        pltpu.make_async_copy(source, target, sems.at[i])
        for i, (source, target) in enumerate(zip(refs[first:count], local, strict=True))
    ]
    for copy in copies:
        copy.start()
    for copy in copies:
        copy.wait()
    body(*refs[:first], *local, *refs[count : -1 - (count - first)])


def call(body, name, args, outs, flops, first=None, scratch=(), specs=()):
    count, scratch = len(args), list(scratch)
    first = count if first is None else first
    if first < count:
        scratch += [pltpu.VMEM(a.shape, a.dtype) for a in args[first:]]
        scratch.append(pltpu.SemaphoreType.DMA((count - first,)))
        args = [
            *args[:first],
            *(pltpu.with_memory_space_constraint(a, pltpu.HBM) for a in args[first:]),
        ]
        if first:
            body = functools.partial(fetched, body, count, first)
    specs = list(specs) + [VMEM] * (first - len(specs)) + [HBM] * (count - first)
    return pl.pallas_call(
        body,
        in_specs=specs,
        out_specs=[VMEM] * len(outs),
        out_shape=outs,
        scratch_shapes=scratch,
        compiler_params=pltpu.CompilerParams(vmem_limit_bytes=24 << 20),
        cost_estimate=pl.CostEstimate(flops=flops, bytes_accessed=4 << 20, transcendentals=0),
        name=name,
    )(*args)


def states(pieces, *args):
    return call(k_states, "states", args, [shape((pieces, 1, 4224))], 1 << 31, 0)[0]


def scan(odd, got):
    out = [shape((got.shape[0], 1, 4096))]
    scratch = [pltpu.VMEM((got.shape[0], 1, COLS), F32)]
    return call(k_scan, "scan", (odd, got), out, 1 << 28, scratch=scratch, specs=[SMEM])[0]


def inner(odd, *args):
    outs = [
        shape((TOK, COLS)), shape((HEADS, TOK)), shape((HEADS, TOK)),
        shape((TOK, STATE)), shape((TOK, STATE)),
        shape((TOK, COLS), BF16), shape((TOK, COLS), BF16),
        shape((TOK, COLS), BF16), shape((TOK, COLS), BF16),
        shape((8, COLS)), shape((STATE, COLS)),
    ]
    scratch = [pltpu.VMEM((TOK, TOK), F32), pltpu.VMEM((TOK, TOK), F32)]
    return call(k_inner, "inner", (odd, *args), outs, 1 << 33, 1, scratch, [SMEM])


def proj(mine, *args):
    body = functools.partial(k_proj, mine)
    name = "kept" if mine else "sent"
    return call(body, name, args, [shape((TOK, STATE))], 1 << 30, specs=[SMEM])[0]


def params(pieces, *args):
    outs = [shape((HEADS, TOK)), shape((pieces, 1, 128))]
    return call(k_params, "params", args, outs, 1 << 30, 1)


def dx(*args):
    return call(k_dx, "dx", args, [shape((TOK, COLS), BF16)], 1 << 30, 1)[0]


def fold(got):
    return call(k_fold, "fold", (got,), [shape(got.shape)], 1 << 20)[0]


def on_device(tokens_x, raw_dt, in_b, in_c, decay_rate, skip_gain, step_bias, grad_y):
    ctx = ("y", "x")
    pieces = lax.axis_size(ctx)
    odd = lax.rem(lax.axis_index(ctx), 2).astype(jnp.int32).reshape(1)
    core = lax.axis_index("c").astype(jnp.int32).reshape(1)
    rate, skip, bias = (a.reshape(1, HEADS) for a in (decay_rate, skip_gain, step_bias))
    data = (tokens_x, grad_y, in_b, in_c, raw_dt, rate, bias)

    send = states(pieces, *data)
    send, odd, core = lax.optimization_barrier((send, odd, core))
    got = lax.all_to_all(send, ctx, 0, 0)
    part, rs, cs, db, dc, xh, xl, gh, gl, sk, state = inner(odd, *data, skip)
    got = lax.all_to_all(scan(odd, got), ctx, 0, 0)
    factors = (core, got, xh, xl, gh, gl, db, dc)
    swap = [(0, 1), (1, 0)]
    mine = lax.ppermute(proj(False, *factors), "c", swap)
    mine = proj(True, *factors) + mine
    grad_raw, partial = params(pieces, got, *data, rs, cs, sk, state)
    ranks = lax.axis_size("z")
    mine = lax.all_to_all(mine.reshape(ranks, TOK // ranks, STATE), "z", 0, 0)
    grad_x = dx(got, part, in_b, raw_dt, rate, bias)
    mine = lax.all_to_all(fold(mine), "z", 0, 0).reshape(TOK, STATE)
    other = lax.ppermute(mine, "c", swap)
    partial = jnp.sum(lax.all_to_all(partial, ctx, 0, 0), axis=(0, 1))
    first = core[0] == 0
    grad_b, grad_c = jnp.where(first, mine, other), jnp.where(first, other, mine)
    return (
        grad_x, grad_raw, grad_b, grad_c,
        partial[:HEADS], partial[2 * HEADS : 3 * HEADS], partial[HEADS : 2 * HEADS],
    )


def solution(mesh):
    fine = Mesh(mesh.devices.reshape(8, 4, 8, 2), ("y", "x", "z", "c"))
    ctx, head = ("y", "x"), ("z", "c")
    return jax.shard_map(
        on_device,
        mesh=fine,
        in_specs=(
            P(ctx, head), P(head, ctx), P(ctx, None), P(ctx, None),
            P(head), P(head), P(head), P(ctx, head),
        ),
        out_specs=(
            P(ctx, head), P(head, ctx), P(ctx, None), P(ctx, None),
            P(head), P(head), P(head),
        ),
        check_vma=False,
    )
```
